32 devices in a mesh: pipe: 2 (over core), heads: 2 (over x), shard: 8 (over z, y).
Axes of the slice: x: 2, y: 2, z: 4, core: 2. Of those that a mesh axis runs over, the one named last changes fastest.
Arguments:
- inputs: bfloat16 [16, 256, 384], P('shard'), may hold values from -6 to 6
- conditioning: bfloat16 [16, 384], P('shard'), may hold values from -6 to 6
- out_grad: float32 [16, 256, 384], P('shard'), may hold values from -6 to 6
- weight_mod: bfloat16 [2, 384, 6, 384], P('pipe', 'shard'), may hold values from -0.3125 to 0.3125
- bias_mod: bfloat16 [2, 6, 384], P('pipe', None, 'shard'), may hold values from -1.796875 to 1.796875
- weight_qkv: bfloat16 [2, 384, 3, 384], P('pipe', 'shard', None, 'heads'), may hold values from -0.3125 to 0.3125
- bias_qv: bfloat16 [2, 2, 384], P('pipe', None, ('heads', 'shard')), may hold values from -3 to 3
- weight_out: bfloat16 [2, 384, 384], P('pipe', 'heads', 'shard'), may hold values from -3 to 3
- bias_out: bfloat16 [2, 384], P('pipe', 'shard'), may hold values from -1.796875 to 1.796875
- first_feed_weight: bfloat16 [2, 384, 1536], P('pipe', 'shard', 'heads'), may hold values from -0.3125 to 0.3125
- first_feed_bias: bfloat16 [2, 1536], P('pipe', ('heads', 'shard')), may hold values from -3 to 3
- second_feed_weight: bfloat16 [2, 1536, 384], P('pipe', 'heads', 'shard'), may hold values from -0.15625 to 0.15625
- second_feed_bias: bfloat16 [2, 384], P('pipe', 'shard'), may hold values from -1.796875 to 1.796875
Outputs:
- activations: bfloat16 [2, 16, 256, 384], P('pipe', 'shard')
- input_grads: float32 [2, 16, 256, 384], P('pipe', 'shard')
- cond_grad: float32 [16, 384], P('shard')
- grad_weight_mod: float32 [2, 384, 6, 384], P('pipe', 'shard')
- grad_bias_mod: float32 [2, 6, 384], P('pipe', None, 'shard')
- grad_weight_qkv: float32 [2, 384, 3, 384], P('pipe', 'shard', None, 'heads')
- grad_bias_qv: float32 [2, 2, 384], P('pipe', None, ('heads', 'shard'))
- grad_weight_out: float32 [2, 384, 384], P('pipe', 'heads', 'shard')
- grad_bias_out: float32 [2, 384], P('pipe', 'shard')
- grad_weight_up: float32 [2, 384, 1536], P('pipe', 'shard', 'heads')
- grad_bias_up: float32 [2, 1536], P('pipe', ('heads', 'shard'))
- grad_weight_down: float32 [2, 1536, 384], P('pipe', 'heads', 'shard')
- grad_bias_down: float32 [2, 384], P('pipe', 'shard')
The draws below stay inside these ranges and needn't reach their ends.
All inputs are finite; a program needn't handle non-finite values.
Results may differ from the reference program's by a relative error of at most 0.024.
Values may be sent and summed in bfloat16 or wider, within the bound.
A program may use at most 128 MiB of HBM per device.

```python
import jax
import jax.numpy as jnp
from jax import lax

D = 384
HD = 64
FF = 1536
SEQ = 256
LATENTS = 16


def level_of(stream_key, dims, pieces, low, high):
    def one(axis_at, parts):
        draws = jax.random.uniform(jax.random.fold_in(jax.random.fold_in(stream_key, 6), axis_at), (parts,), jnp.float32, low / len(pieces), high / len(pieces))
        return jnp.repeat(jnp.exp(draws), dims[axis_at] // parts).reshape((-1,) + (1,) * (len(dims) - axis_at - 1))

    factor_of = one(*pieces[0])
    for cut in pieces[1:]:
        factor_of = factor_of * one(*cut)
    return factor_of


def noise(own_key, extent, width, bound, split=(), held_as=jnp.bfloat16):
    factor_of = level_of(own_key, extent, split, -0.22, 0.18) if split else 1.0
    entries = jax.random.normal(own_key, extent, jnp.float32) * width * factor_of
    return jnp.minimum(jnp.maximum(entries, -bound), bound).astype(held_as)


def setup_inputs(seed: int = 0) -> dict:
    seeds = jax.random.split(jax.random.key(seed), 14)
    return {
        "inputs": noise(seeds[0], (LATENTS, SEQ, D), 1.0, 6.0, ((0, 8),)),
        "conditioning": noise(seeds[1], (LATENTS, D), 1.0, 6.0, ((0, 8),)),
        "out_grad": noise(seeds[2], (LATENTS, SEQ, D), 1.0, 6.0, ((0, 8),), jnp.float32),
        "weight_mod": noise(seeds[3], (2, D, 6, D), D ** -0.5, 0.3125, ((0, 2), (1, 8))),
        "bias_mod": noise(seeds[4], (2, 6, D), 0.3, 1.796875, ((0, 2), (2, 8))),
        "weight_qkv": noise(seeds[5], (2, D, 3, D), D ** -0.5, 0.3125, ((0, 2), (1, 8), (3, 2))),
        "bias_qv": noise(seeds[6], (2, 2, D), 0.5, 3.0, ((0, 2), (2, 16))),
        "weight_out": noise(seeds[7], (2, D, D), 4 ** -0.5, 3.0, ((0, 2), (1, 2), (2, 8))),
        "bias_out": noise(seeds[8], (2, D), 0.3, 1.796875, ((0, 2), (1, 8))),
        "first_feed_weight": noise(seeds[9], (2, D, FF), D ** -0.5, 0.3125, ((0, 2), (1, 8), (2, 2))),
        "first_feed_bias": noise(seeds[10], (2, FF), 0.5, 3.0, ((0, 2), (1, 16))),
        "second_feed_weight": noise(seeds[11], (2, FF, D), FF ** -0.5, 0.15625, ((0, 2), (1, 2), (2, 8))),
        "second_feed_bias": noise(seeds[12], (2, D), 0.3, 1.796875, ((0, 2), (1, 8))),
    }


@jax.custom_vjp
def low(v):
    return lax.optimization_barrier(v.astype(jnp.bfloat16)).astype(jnp.float32)

@jax.custom_vjp
def low_back(v):
    return v

def low_keep(v):
    return (low(v), None)

def low_pass(kept, grad):
    return (grad,)

def back_keep(v):
    return (v, None)

def back_low(kept, grad):
    return (low(grad),)
low.defvjp(low_keep, low_pass)
low_back.defvjp(back_keep, back_low)

def norm_rows(values):
    average = lax.optimization_barrier(jnp.mean(values, axis=-1, keepdims=True))
    centered = values - average
    variance = lax.optimization_barrier(jnp.mean(centered * centered, axis=-1, keepdims=True))
    return centered * lax.rsqrt(variance + 1e-06)

def block(entering, condition, weight_mod, bias_mod, weight_qkv, bias_qv, weight_out, bias_out, first_feed_weight, first_feed_bias, second_feed_weight, second_feed_bias):
    max_precision_setting = lax.Precision.HIGHEST
    latents, length, model_width = entering.shape
    cond_act = low(jax.nn.silu(condition))
    modulation = low_back(jnp.einsum('ld,dke->lke', cond_act, weight_mod, precision=max_precision_setting) + bias_mod)
    mod_rows = [modulation[:, column][:, None, :] for column in range(6)]
    normed = low(norm_rows(entering) * (1.0 + mod_rows[1]) + mod_rows[0])
    projected = jnp.einsum('lsd,dke->lske', normed, weight_qkv, precision=max_precision_setting)
    queries = projected[:, :, 0] + bias_qv[0]
    key_rows = projected[:, :, 1]
    values = projected[:, :, 2] + bias_qv[1]
    joined = low_back(low(jnp.stack([queries, key_rows, values], axis=2)))
    split_heads = joined.reshape(latents, length, 3, model_width // HD, HD)
    scores = low_back(jnp.einsum('lqhe,lkhe->lhqk', split_heads[:, :, 0], split_heads[:, :, 1], precision=max_precision_setting) * HD ** (-0.5))
    attn_probs = low(jax.nn.softmax(scores, axis=-1))
    mixed_heads = jnp.einsum('lhqk,lkhe->lqhe', attn_probs, split_heads[:, :, 2], precision=max_precision_setting)
    mixed_heads = low_back(low(mixed_heads.reshape(latents, length, model_width)))
    attended = low_back(jnp.einsum('lse,ed->lsd', mixed_heads, weight_out, precision=max_precision_setting) + bias_out)
    hidden = entering + mod_rows[2] * attended
    second_normalized = low(norm_rows(hidden) * (1.0 + mod_rows[4]) + mod_rows[3])
    raised_hidden = low_back(jnp.einsum('ikx,xc->ikc', second_normalized, first_feed_weight, precision=max_precision_setting) + first_feed_bias)
    hidden_activated = low(jax.nn.gelu(raised_hidden, approximate=True))
    lowered_output = low_back(jnp.einsum('vua,ap->vup', hidden_activated, second_feed_weight, precision=max_precision_setting) + second_feed_bias)
    return hidden + mod_rows[5] * lowered_output

def reference(inputs, conditioning, out_grad, weight_mod, bias_mod, weight_qkv, bias_qv, weight_out, bias_out, first_feed_weight, first_feed_bias, second_feed_weight, second_feed_bias):
    params = [matrix.astype(jnp.float32) for matrix in (weight_mod, bias_mod, weight_qkv, bias_qv, weight_out, bias_out, first_feed_weight, first_feed_bias, second_feed_weight, second_feed_bias)]
    section_zero = [matrix[0] for matrix in params]
    section_one = [matrix[1] for matrix in params]
    group_count = LATENTS // 16

    def grouped(array):
        return array.reshape((group_count, 16) + array.shape[1:])

    def one_group(totals, batch):
        block_in = batch[0].astype(jnp.float32)
        cond_in = batch[1].astype(jnp.float32)
        grad_in = batch[2].astype(jnp.float32)
        first_out, pull_first = jax.vjp(block, block_in, cond_in, *section_zero)
        sent = low(first_out)
        second_out, pull_second = jax.vjp(block, sent, cond_in, *section_one)
        grads_second = pull_second(grad_in)
        grads_first = pull_first(low(grads_second[0]))
        totals = jax.tree.map(jnp.add, totals, (tuple(grads_first[2:]), tuple(grads_second[2:])))
        produced = (jnp.stack([sent, second_out]).astype(jnp.bfloat16), jnp.stack([grads_first[0], grads_second[0]]), grads_first[1] + grads_second[1])
        return (totals, produced)
    zeros_each = tuple((jnp.zeros_like(matrix) for matrix in section_zero))
    totals, produced = lax.scan(one_group, (zeros_each, zeros_each), (grouped(inputs), grouped(conditioning), grouped(out_grad)))
    activations = jnp.transpose(produced[0], (1, 0, 2, 3, 4)).reshape(2, LATENTS, SEQ, D)
    input_grads = jnp.transpose(produced[1], (1, 0, 2, 3, 4)).reshape(2, LATENTS, SEQ, D)
    cond_grad = produced[2].reshape(LATENTS, D)
    stacked = [jnp.stack([early_grad, late_grad]) for early_grad, late_grad in zip(totals[0], totals[1])]
    return (activations, input_grads, cond_grad, stacked[0], stacked[1], stacked[2], stacked[3], stacked[4], stacked[5], stacked[6], stacked[7], stacked[8], stacked[9])
```

```python
import math

import jax
import jax.numpy as jnp
from jax import lax
from jax.experimental import pallas as pl
from jax.experimental.pallas import tpu as pltpu
from jax.sharding import PartitionSpec as P

HD = 64
D = 384
EH = 192
FH = 768
QKV = 3 * EH
COLS = QKV + EH + 2 * FH
MODH = 3 * D
PAD = 128
WIDE = COLS + MODH + PAD
BIAS_COLS = 11
SCALING = HD**-0.5
SMALL = 6 * D + 2 * QKV + D + 2 * FH + D + D + D
BF = jnp.bfloat16
F32 = jnp.float32


def dot_nn(a, b):
    return lax.dot_general(a, b, (((1,), (0,)), ((), ())), preferred_element_type=F32)


def dot_nt(a, b):
    return lax.dot_general(a, b, (((1,), (1,)), ((), ())), preferred_element_type=F32)


def dot_tn(a, b):
    return lax.dot_general(a, b, (((0,), (0,)), ((), ())), preferred_element_type=F32)


def rows_mean(v):
    return jnp.mean(v, axis=-1, keepdims=True)


def norm_rows(v):
    centered = v - rows_mean(v)
    inverse = lax.rsqrt(rows_mean(centered * centered) + 1e-06)
    return centered * inverse, inverse


def norm_back(e, normed, inverse):
    return inverse * (e - rows_mean(e) - normed * rows_mean(e * normed))


def token_sum(v):
    return jnp.sum(v, axis=0, keepdims=True)


def block_kernel(
    latents,
    place,
    x_ref,
    cond_ref,
    g_ref,
    w_ref,
    bm_ref,
    bqkv_ref,
    bo_ref,
    bu_ref,
    bd_ref,
    act_out,
    grad_out,
    dw_out,
    small_out,
    n1_s,
    inv1_s,
    normed_s,
    qkv_s,
    probs_s,
    mixed_s,
    attended_s,
    n2_s,
    inv2_s,
    normed_two_s,
    slope_s,
    activated_s,
    down_s,
    mod_s,
    upg_s,
    pjg_s,
    back_s,
    dw_s,
):
    section = place[0]
    cond = cond_ref[0]
    sig = jax.nn.sigmoid(cond)
    cond_act = (cond * sig).astype(BF)
    cond_rows = jnp.broadcast_to(cond_act, (16, D))

    def weight(s, h, a, b):
        return w_ref[s, h, :, a:b]

    def forward(s, x):
        for h in range(2):
            rows = dot_nn(cond_rows, weight(s, h, COLS, COLS + MODH))[0:1]
            mod_s[s, 0:1, h * MODH : (h + 1) * MODH] = rows + bm_ref[s, :, h * MODH : (h + 1) * MODH]
        shift1, scale1, gate1, shift2, scale2, gate2 = (
            mod_s[s, 0:1, i * D : (i + 1) * D] for i in range(6)
        )
        n1, inv1 = norm_rows(x)
        n1_s[s] = n1
        inv1_s[s] = inv1
        normed = (n1 * (1.0 + scale1) + shift1).astype(BF)
        normed_s[s] = normed
        attended = jnp.broadcast_to(bo_ref[s], x.shape)
        for h in range(2):
            qkv = (dot_nn(normed, weight(s, h, 0, QKV)) + bqkv_ref[s, h]).astype(BF)
            qkv_s[s, h] = qkv
            mixed = []
            for i in range(3):
                q, k, v = (qkv[:, j * EH + i * HD : j * EH + (i + 1) * HD] for j in range(3))
                scores = dot_nt(q, k) * SCALING
                expo = jnp.exp(scores - jnp.max(scores, axis=-1, keepdims=True))
                probs = expo / jnp.sum(expo, axis=-1, keepdims=True)
                probs_s[s, 3 * h + i] = probs
                mixed.append(dot_nn(probs.astype(BF), v))
            mixed = jnp.concatenate(mixed, axis=1).astype(BF)
            mixed_s[s, h] = mixed
            attended = attended + dot_nt(mixed, weight(s, h, QKV, QKV + EH))
        attended_s[s] = attended
        hidden = x + gate1 * attended
        n2, inv2 = norm_rows(hidden)
        n2_s[s] = n2
        inv2_s[s] = inv2
        normed_two = (n2 * (1.0 + scale2) + shift2).astype(BF)
        normed_two_s[s] = normed_two
        down = jnp.broadcast_to(bd_ref[s], x.shape)
        at = QKV + EH
        for h in range(2):
            up = dot_nn(normed_two, weight(s, h, at, at + FH)) + bu_ref[s, h]
            c = math.sqrt(2.0 / math.pi)
            square = up * up
            tanh = jnp.tanh(c * (up + 0.044715 * (square * up)))
            half = 0.5 * (1.0 + tanh)
            activated = (up * half).astype(BF)
            activated_s[s, h] = activated
            slope_s[s, h] = half + (0.5 * c) * up * (1.0 - tanh * tanh) * (
                1.0 + (3 * 0.044715) * square
            )
            down = down + dot_nt(activated, weight(s, h, at + FH, at + 2 * FH))
        down_s[s] = down
        return hidden + gate2 * down

    def add_weight(h, a, b, value):
        if latents == 1:
            dw_out[h, :, a:b] = value.astype(BF)
        else:
            dw_s[h, :, a:b] += value

    def backward(s, g):
        shift1, scale1, gate1, shift2, scale2, gate2 = (
            mod_s[s, 0:1, i * D : (i + 1) * D] for i in range(6)
        )
        at = QKV + EH
        down_grad = (gate2 * g).astype(BF)
        n2_grad = None
        for h in range(2):
            active_grad = dot_nn(down_grad, weight(s, h, at + FH, at + 2 * FH))
            up_grad = (active_grad * slope_s[s, h]).astype(BF)
            upg_s[h] = up_grad
            part = dot_nt(up_grad, weight(s, h, at, at + FH))
            n2_grad = part if n2_grad is None else n2_grad + part
        n2 = n2_s[s]
        hidden_grad = g + norm_back(n2_grad * (1.0 + scale2), n2, inv2_s[s])
        attend_grad = (gate1 * hidden_grad).astype(BF)
        n1_grad = None
        for h in range(2):
            mixed_grad = dot_nn(attend_grad, weight(s, h, QKV, QKV + EH)).astype(BF)
            qkv = qkv_s[s, h]
            parts = [[], [], []]
            for i in range(3):
                q, k, v = (qkv[:, j * EH + i * HD : j * EH + (i + 1) * HD] for j in range(3))
                mg = mixed_grad[:, i * HD : (i + 1) * HD]
                probs = probs_s[s, 3 * h + i]
                parts[2].append(dot_tn(probs.astype(BF), mg))
                weighted = probs * dot_nt(mg, v)
                score_grad = (
                    weighted - probs * jnp.sum(weighted, axis=-1, keepdims=True)
                ).astype(BF)
                parts[0].append(dot_nn(score_grad, k) * SCALING)
                parts[1].append(dot_tn(score_grad, q) * SCALING)
            proj_grad = jnp.concatenate(parts[0] + parts[1] + parts[2], axis=1).astype(BF)
            pjg_s[h] = proj_grad
            part = dot_nt(proj_grad, weight(s, h, 0, QKV))
            n1_grad = part if n1_grad is None else n1_grad + part
        n1 = n1_s[s]
        input_grad = hidden_grad + norm_back(n1_grad * (1.0 + scale1), n1, inv1_s[s])
        back_s[...] = input_grad

        @pl.when(section == s)
        def _():
            grad_out[0] = input_grad
            mod_grad = jnp.concatenate(
                [
                    token_sum(n1_grad),
                    token_sum(n1_grad * n1),
                    token_sum(hidden_grad * attended_s[s]),
                    token_sum(n2_grad),
                    token_sum(n2_grad * n2),
                    token_sum(g * down_s[s]),
                ],
                axis=1,
            ).astype(BF)
            mod_rows = jnp.broadcast_to(mod_grad, (16, 6 * D))
            silu_grad = sum(
                dot_nt(
                    mod_rows[:, h * MODH : (h + 1) * MODH], weight(s, h, COLS, COLS + MODH)
                )[0:1]
                for h in range(2)
            )
            cond_grad = silu_grad * (sig * (1.0 + cond * (1.0 - sig)))
            pieces = [mod_grad.astype(F32)]
            pieces += [token_sum(pjg_s[h].astype(F32)) for h in range(2)]
            pieces += [token_sum(attend_grad.astype(F32))]
            pieces += [token_sum(upg_s[h].astype(F32)) for h in range(2)]
            pieces += [token_sum(down_grad.astype(F32)), cond_grad, cond_act.astype(F32)]
            small_out[0] = jnp.concatenate(pieces, axis=1)
            for h in range(2):
                add_weight(h, 0, QKV, dot_tn(normed_s[s], pjg_s[h]))
                add_weight(h, QKV, at, dot_tn(attend_grad, mixed_s[s, h]))
                add_weight(h, at, at + FH, dot_tn(normed_two_s[s], upg_s[h]))
                add_weight(h, at + FH, at + 2 * FH, dot_tn(down_grad, activated_s[s, h]))

    if latents > 1:

        @pl.when(pl.program_id(0) == 0)
        def _():
            dw_s[...] = jnp.zeros_like(dw_s)

    y0 = forward(0, x_ref[0].astype(F32)).astype(BF)

    @pl.when(section == 0)
    def _():
        act_out[0] = y0

    y1 = forward(1, y0.astype(F32))

    @pl.when(section == 1)
    def _():
        act_out[0] = y1.astype(BF)

    backward(1, g_ref[0])

    @pl.when(section == 0)
    def _():
        backward(0, back_s[...].astype(BF).astype(F32))

    if latents > 1:

        @pl.when(pl.program_id(0) == latents - 1)
        def _():
            dw_out[...] = dw_s[...].astype(BF)


def run_blocks(place, x, cond, g, w, bm, bqkv, bo, bu, bd, latents):
    length = x.shape[1]

    def picked(shape):
        return pl.BlockSpec(
            (1,) + shape, lambda i, place: (place[1] * latents + i,) + (0,) * len(shape)
        )

    def own(shape):
        return pl.BlockSpec((1,) + shape, lambda i, place: (i,) + (0,) * len(shape))

    def whole(a):
        return pl.BlockSpec(
            a.shape, lambda i, place: (0,) * a.ndim, pipeline_mode=pl.Buffered(1)
        )

    def kept(shape, dtype):
        return pltpu.VMEM(shape, dtype)

    def kernel(*refs):
        block_kernel(latents, *refs)

    t = length
    return pl.pallas_call(
        kernel,
        grid_spec=pltpu.PrefetchScalarGridSpec(
            num_scalar_prefetch=1,
            grid=(latents,),
            in_specs=[picked((t, D)), picked((1, D)), picked((t, D))]
            + [whole(a) for a in (w, bm, bqkv, bo, bu, bd)],
            out_specs=[
                own((t, D)),
                own((t, D)),
                pl.BlockSpec((2, D, COLS), lambda i, place: (0, 0, 0)),
                own((1, SMALL)),
            ],
            scratch_shapes=[
                kept((2, t, D), F32),
                kept((2, t, 1), F32),
                kept((2, t, D), BF),
                kept((2, 2, t, QKV), BF),
                kept((2, 6, t, t), F32),
                kept((2, 2, t, EH), BF),
                kept((2, t, D), F32),
                kept((2, t, D), F32),
                kept((2, t, 1), F32),
                kept((2, t, D), BF),
                kept((2, 2, t, FH), F32),
                kept((2, 2, t, FH), BF),
                kept((2, t, D), F32),
                kept((2, 8, 6 * D), F32),
                kept((2, t, FH), BF),
                kept((2, t, QKV), BF),
                kept((t, D), F32),
                kept((2, D, COLS) if latents > 1 else (8, 128), F32),
            ],
        ),
        out_shape=(
            jax.ShapeDtypeStruct((latents, t, D), BF),
            jax.ShapeDtypeStruct((latents, t, D), F32),
            jax.ShapeDtypeStruct((2, D, COLS), BF),
            jax.ShapeDtypeStruct((latents, 1, SMALL), F32),
        ),
        compiler_params=pltpu.CompilerParams(vmem_limit_bytes=58 * 1024 * 1024),
        cost_estimate=pl.CostEstimate(
            flops=12_000_000_000, bytes_accessed=16_000_000, transcendentals=2_000_000
        ),
    )(place, x, cond, g, w, bm, bqkv, bo, bu, bd)


def swapped(value, axis):
    return lax.ppermute(value, axis, [(0, 1), (1, 0)])


def both_halves(mine, other, half):
    first = jnp.where(half == 0, mine, other)
    second = jnp.where(half == 0, other, mine)
    return jnp.concatenate([first, second], axis=0)


def per_device(
    inputs,
    conditioning,
    out_grad,
    weight_mod,
    bias_mod,
    weight_qkv,
    bias_qv,
    weight_out,
    bias_out,
    first_feed_weight,
    first_feed_bias,
    second_feed_weight,
    second_feed_bias,
):
    section = lax.axis_index("pipe")
    half = lax.axis_index("heads")
    shard = lax.axis_index("shard")
    shards = lax.axis_size("shard")
    rows = weight_qkv.shape[1]
    latents = inputs.shape[0] // 2

    own_mod = lax.dynamic_slice_in_dim(weight_mod[0].reshape(rows, 2 * MODH), half * MODH, MODH, 1)
    own_bias = jnp.concatenate(
        [
            bias_mod.reshape(-1),
            bias_qv.reshape(-1),
            bias_out.reshape(-1),
            first_feed_bias.reshape(-1),
            second_feed_bias.reshape(-1),
        ]
    ).reshape(rows, BIAS_COLS)
    packed = jnp.concatenate(
        [
            weight_qkv.reshape(rows, QKV),
            weight_out[0].T,
            first_feed_weight[0],
            second_feed_weight[0].T,
            own_mod,
            own_bias,
            jnp.zeros((rows, PAD - BIAS_COLS), BF),
        ],
        axis=1,
    )
    gathered = gather_weights(packed)
    w = gathered.reshape(2, 2, shards * rows, WIDE)
    bias = (
        w[:, :, :, COLS + MODH : COLS + MODH + BIAS_COLS]
        .astype(F32)
        .reshape(2, 2, shards, rows * BIAS_COLS)
    )
    own_qv, own_up = EH // shards, FH // shards
    cut = [6 * rows, 2 * own_qv, rows, own_up, rows]
    ends = [sum(cut[: i + 1]) for i in range(5)]
    bm, bqv, bo, bu, bd = jnp.split(bias, ends[:-1], axis=-1)
    bm = bm[:, 0].reshape(2, shards, 6, rows).swapaxes(1, 2).reshape(2, 1, 6 * D)
    bqv = bqv.reshape(2, 2, shards, 2, own_qv).swapaxes(2, 3).reshape(2, 2, 2, EH)
    bqkv = jnp.concatenate([bqv[:, :, :1], jnp.zeros_like(bqv[:, :, :1]), bqv[:, :, 1:]], axis=2)
    bqkv = bqkv.reshape(2, 2, 1, QKV)
    bo = bo[:, 0].reshape(2, 1, D)
    bu = bu.reshape(2, 2, 1, FH)
    bd = bd[:, 0].reshape(2, 1, D)

    place = jnp.stack([section, half]).astype(jnp.int32)
    act, grad, dw, small = run_blocks(
        place,
        inputs,
        conditioning.astype(F32)[:, None, :],
        out_grad,
        w,
        bm,
        bqkv,
        bo,
        bu,
        bd,
        latents,
    )
    activations = both_halves(act, swapped(act, "heads"), half)[None]
    other_grad = swapped(grad.astype(BF), "heads").astype(F32)
    input_grads = both_halves(grad, other_grad, half)[None]

    small = jnp.broadcast_to(small.reshape(1, latents * SMALL), (4 * shards, latents * SMALL))
    small = lax.all_to_all(small, ("pipe", "heads", "shard"), 0, 0, tiled=True)
    small = small.reshape(2, 2, shards, latents, SMALL)
    cond_at = SMALL - 2 * D
    cond_grad = lax.dynamic_index_in_dim(small, shard, 2, keepdims=False)
    cond_grad = cond_grad[..., cond_at : cond_at + D].sum(axis=0).reshape(2 * latents, D)
    mine = lax.dynamic_index_in_dim(small, section, 0, keepdims=False).reshape(-1, SMALL)
    mod_grad = mine[:, : 6 * D].astype(BF)
    cond_act = lax.dynamic_slice_in_dim(mine[:, SMALL - D :], shard * rows, rows, 1).astype(BF)
    grad_mod = dot_tn(cond_act, mod_grad).reshape(1, rows, 6, D)
    sums = mine[:, : cond_at].sum(axis=0)
    grad_bias_mod = lax.dynamic_slice_in_dim(sums[: 6 * D].reshape(6, D), shard * rows, rows, 1)
    at = 6 * D
    proj = sums[at : at + 2 * QKV].reshape(2, 3, EH)
    proj = lax.dynamic_index_in_dim(proj, half, 0, keepdims=False)
    proj = lax.dynamic_slice_in_dim(proj, shard * own_qv, own_qv, 1)
    grad_bias_qv = jnp.stack([proj[0], proj[2]])
    at += 2 * QKV
    grad_bias_out = lax.dynamic_slice_in_dim(sums, at + shard * rows, rows)
    at += D
    grad_bias_up = lax.dynamic_slice_in_dim(sums, at + half * FH + shard * own_up, own_up)
    at += 2 * FH
    grad_bias_down = lax.dynamic_slice_in_dim(sums, at + shard * rows, rows)

    total = reduce_weights(dw.reshape(2, shards, rows, COLS))
    at = QKV + EH
    return (
        activations,
        input_grads,
        cond_grad,
        grad_mod,
        grad_bias_mod[None],
        total[:, :QKV].reshape(1, rows, 3, EH),
        grad_bias_qv[None],
        total[:, QKV:at].T[None],
        grad_bias_out[None],
        total[:, at : at + FH][None],
        grad_bias_up[None],
        total[:, at + FH :].T[None],
        grad_bias_down[None],
    )


def gather_weights(packed):
    return lax.all_gather(packed, ("pipe", "heads", "shard"))


def reduce_weights(dw):
    tiles = dw.reshape(-1, *dw.shape[2:])
    arrived = lax.all_to_all(tiles, ("heads", "shard"), 0, 0, tiled=True)
    return arrived.astype(F32).sum(axis=0)


def solution(mesh):
    return jax.shard_map(
        per_device,
        mesh=mesh,
        in_specs=(
            P("shard", None, None),
            P("shard", None),
            P("shard", None, None),
            P("pipe", "shard", None, None),
            P("pipe", None, "shard"),
            P("pipe", "shard", None, "heads"),
            P("pipe", None, ("heads", "shard")),
            P("pipe", "heads", "shard"),
            P("pipe", "shard"),
            P("pipe", "shard", "heads"),
            P("pipe", ("heads", "shard")),
            P("pipe", "heads", "shard"),
            P("pipe", "shard"),
        ),
        out_specs=(
            P("pipe", "shard", None, None),
            P("pipe", "shard", None, None),
            P("shard", None),
            P("pipe", "shard", None, None),
            P("pipe", None, "shard"),
            P("pipe", "shard", None, "heads"),
            P("pipe", None, ("heads", "shard")),
            P("pipe", "heads", "shard"),
            P("pipe", "shard"),
            P("pipe", "shard", "heads"),
            P("pipe", ("heads", "shard")),
            P("pipe", "heads", "shard"),
            P("pipe", "shard"),
        ),
        check_vma=False,
    )
```

```python
import math

import jax
import jax.numpy as jnp
from jax import lax
from jax.experimental import pallas as pl
from jax.experimental.pallas import tpu as pltpu
from jax.sharding import PartitionSpec as P

HD = 64
D = 384
EH = 192
FH = 768
QKV = 3 * EH
COLS = QKV + EH + 2 * FH
MODH = 3 * D
PAD = 128
WIDE = COLS + MODH + PAD
BIAS_COLS = 11
SCALING = HD**-0.5
SMALL = 6 * D + 2 * QKV + D + 2 * FH + D + D + D
BF = jnp.bfloat16
F32 = jnp.float32


def dot_nn(a, b):
    return lax.dot_general(a, b, (((1,), (0,)), ((), ())), preferred_element_type=F32)


def dot_nt(a, b):
    return lax.dot_general(a, b, (((1,), (1,)), ((), ())), preferred_element_type=F32)


def dot_tn(a, b):
    return lax.dot_general(a, b, (((0,), (0,)), ((), ())), preferred_element_type=F32)


def rows_mean(v):
    return jnp.mean(v, axis=-1, keepdims=True)


def norm_rows(v):
    centered = v - rows_mean(v)
    inverse = lax.rsqrt(rows_mean(centered * centered) + 1e-06)
    return centered * inverse, inverse


def norm_back(e, normed, inverse):
    return inverse * (e - rows_mean(e) - normed * rows_mean(e * normed))


def token_sum(v):
    return jnp.sum(v, axis=0, keepdims=True)


def block_kernel(
    latents,
    place,
    x_ref,
    cond_ref,
    g_ref,
    w_ref,
    bm_ref,
    bqkv_ref,
    bo_ref,
    bu_ref,
    bd_ref,
    act_out,
    grad_out,
    dw_out,
    small_out,
    n1_s,
    inv1_s,
    normed_s,
    qkv_s,
    probs_s,
    mixed_s,
    attended_s,
    n2_s,
    inv2_s,
    normed_two_s,
    slope_s,
    activated_s,
    down_s,
    mod_s,
    upg_s,
    pjg_s,
    back_s,
    dw_s,
):
    section = place[0]
    cond = cond_ref[0]
    sig = jax.nn.sigmoid(cond)
    cond_act = (cond * sig).astype(BF)
    cond_rows = jnp.broadcast_to(cond_act, (16, D))

    def weight(s, h, a, b):
        return w_ref[s, h, :, a:b]

    def forward(s, x):
        for h in range(2):
            rows = dot_nn(cond_rows, weight(s, h, COLS, COLS + MODH))[0:1]
            mod_s[s, 0:1, h * MODH : (h + 1) * MODH] = rows + bm_ref[s, :, h * MODH : (h + 1) * MODH]
        shift1, scale1, gate1, shift2, scale2, gate2 = (
            mod_s[s, 0:1, i * D : (i + 1) * D] for i in range(6)
        )
        n1, inv1 = norm_rows(x)
        n1_s[s] = n1
        inv1_s[s] = inv1
        normed = (n1 * (1.0 + scale1) + shift1).astype(BF)
        normed_s[s] = normed
        attended = jnp.broadcast_to(bo_ref[s], x.shape)
        for h in range(2):
            qkv = (dot_nn(normed, weight(s, h, 0, QKV)) + bqkv_ref[s, h]).astype(BF)
            qkv_s[s, h] = qkv
            mixed = []
            for i in range(3):
                q, k, v = (qkv[:, j * EH + i * HD : j * EH + (i + 1) * HD] for j in range(3))
                scores = dot_nt(q, k) * SCALING
                expo = jnp.exp(scores - jnp.max(scores, axis=-1, keepdims=True))
                probs = expo / jnp.sum(expo, axis=-1, keepdims=True)
                probs_s[s, 3 * h + i] = probs
                mixed.append(dot_nn(probs.astype(BF), v))
            mixed = jnp.concatenate(mixed, axis=1).astype(BF)
            mixed_s[s, h] = mixed
            attended = attended + dot_nt(mixed, weight(s, h, QKV, QKV + EH))
        attended_s[s] = attended
        hidden = x + gate1 * attended
        n2, inv2 = norm_rows(hidden)
        n2_s[s] = n2
        inv2_s[s] = inv2
        normed_two = (n2 * (1.0 + scale2) + shift2).astype(BF)
        normed_two_s[s] = normed_two
        down = jnp.broadcast_to(bd_ref[s], x.shape)
        at = QKV + EH
        for h in range(2):
            up = dot_nn(normed_two, weight(s, h, at, at + FH)) + bu_ref[s, h]
            c = math.sqrt(2.0 / math.pi)
            square = up * up
            tanh = jnp.tanh(c * (up + 0.044715 * (square * up)))
            half = 0.5 * (1.0 + tanh)
            activated = (up * half).astype(BF)
            activated_s[s, h] = activated
            slope_s[s, h] = half + (0.5 * c) * up * (1.0 - tanh * tanh) * (
                1.0 + (3 * 0.044715) * square
            )
            down = down + dot_nt(activated, weight(s, h, at + FH, at + 2 * FH))
        down_s[s] = down
        return hidden + gate2 * down

    def add_weight(h, a, b, value):
        if latents == 1:
            dw_out[h, :, a:b] = value.astype(BF)
        else:
            dw_s[h, :, a:b] += value

    def backward(s, g):
        shift1, scale1, gate1, shift2, scale2, gate2 = (
            mod_s[s, 0:1, i * D : (i + 1) * D] for i in range(6)
        )
        at = QKV + EH
        down_grad = (gate2 * g).astype(BF)
        n2_grad = None
        for h in range(2):
            active_grad = dot_nn(down_grad, weight(s, h, at + FH, at + 2 * FH))
            up_grad = (active_grad * slope_s[s, h]).astype(BF)
            upg_s[h] = up_grad
            part = dot_nt(up_grad, weight(s, h, at, at + FH))
            n2_grad = part if n2_grad is None else n2_grad + part
        n2 = n2_s[s]
        hidden_grad = g + norm_back(n2_grad * (1.0 + scale2), n2, inv2_s[s])
        attend_grad = (gate1 * hidden_grad).astype(BF)
        n1_grad = None
        for h in range(2):
            mixed_grad = dot_nn(attend_grad, weight(s, h, QKV, QKV + EH)).astype(BF)
            qkv = qkv_s[s, h]
            parts = [[], [], []]
            for i in range(3):
                q, k, v = (qkv[:, j * EH + i * HD : j * EH + (i + 1) * HD] for j in range(3))
                mg = mixed_grad[:, i * HD : (i + 1) * HD]
                probs = probs_s[s, 3 * h + i]
                parts[2].append(dot_tn(probs.astype(BF), mg))
                weighted = probs * dot_nt(mg, v)
                score_grad = (
                    weighted - probs * jnp.sum(weighted, axis=-1, keepdims=True)
                ).astype(BF)
                parts[0].append(dot_nn(score_grad, k) * SCALING)
                parts[1].append(dot_tn(score_grad, q) * SCALING)
            proj_grad = jnp.concatenate(parts[0] + parts[1] + parts[2], axis=1).astype(BF)
            pjg_s[h] = proj_grad
            part = dot_nt(proj_grad, weight(s, h, 0, QKV))
            n1_grad = part if n1_grad is None else n1_grad + part
        n1 = n1_s[s]
        input_grad = hidden_grad + norm_back(n1_grad * (1.0 + scale1), n1, inv1_s[s])
        back_s[...] = input_grad

        @pl.when(section == s)
        def _():
            grad_out[0] = input_grad
            mod_grad = jnp.concatenate(
                [
                    token_sum(n1_grad),
                    token_sum(n1_grad * n1),
                    token_sum(hidden_grad * attended_s[s]),
                    token_sum(n2_grad),
                    token_sum(n2_grad * n2),
                    token_sum(g * down_s[s]),
                ],
                axis=1,
            ).astype(BF)
            mod_rows = jnp.broadcast_to(mod_grad, (16, 6 * D))
            silu_grad = sum(
                dot_nt(
                    mod_rows[:, h * MODH : (h + 1) * MODH], weight(s, h, COLS, COLS + MODH)
                )[0:1]
                for h in range(2)
            )
            cond_grad = silu_grad * (sig * (1.0 + cond * (1.0 - sig)))
            pieces = [mod_grad.astype(F32)]
            pieces += [token_sum(pjg_s[h].astype(F32)) for h in range(2)]
            pieces += [token_sum(attend_grad.astype(F32))]
            pieces += [token_sum(upg_s[h].astype(F32)) for h in range(2)]
            pieces += [token_sum(down_grad.astype(F32)), cond_grad, cond_act.astype(F32)]
            small_out[0] = jnp.concatenate(pieces, axis=1)
            for h in range(2):
                add_weight(h, 0, QKV, dot_tn(normed_s[s], pjg_s[h]))
                add_weight(h, QKV, at, dot_tn(attend_grad, mixed_s[s, h]))
                add_weight(h, at, at + FH, dot_tn(normed_two_s[s], upg_s[h]))
                add_weight(h, at + FH, at + 2 * FH, dot_tn(down_grad, activated_s[s, h]))

    if latents > 1:

        @pl.when(pl.program_id(0) == 0)
        def _():
            dw_s[...] = jnp.zeros_like(dw_s)

    y0 = forward(0, x_ref[0].astype(F32)).astype(BF)

    @pl.when(section == 0)
    def _():
        act_out[0] = y0

    y1 = forward(1, y0.astype(F32))

    @pl.when(section == 1)
    def _():
        act_out[0] = y1.astype(BF)

    backward(1, g_ref[0])

    @pl.when(section == 0)
    def _():
        backward(0, back_s[...].astype(BF).astype(F32))

    if latents > 1:

        @pl.when(pl.program_id(0) == latents - 1)
        def _():
            dw_out[...] = dw_s[...].astype(BF)


def run_blocks(place, x, cond, g, w, bm, bqkv, bo, bu, bd, latents):
    length = x.shape[1]

    def picked(shape):
        return pl.BlockSpec(
            (1,) + shape, lambda i, place: (place[1] * latents + i,) + (0,) * len(shape)
        )

    def own(shape):
        return pl.BlockSpec((1,) + shape, lambda i, place: (i,) + (0,) * len(shape))

    def whole(a):
        return pl.BlockSpec(
            a.shape, lambda i, place: (0,) * a.ndim, pipeline_mode=pl.Buffered(1)
        )

    def kept(shape, dtype):
        return pltpu.VMEM(shape, dtype)

    def kernel(*refs):
        block_kernel(latents, *refs)

    t = length
    return pl.pallas_call(
        kernel,
        grid_spec=pltpu.PrefetchScalarGridSpec(
            num_scalar_prefetch=1,
            grid=(latents,),
            in_specs=[picked((t, D)), picked((1, D)), picked((t, D))]
            + [whole(a) for a in (w, bm, bqkv, bo, bu, bd)],
            out_specs=[
                own((t, D)),
                own((t, D)),
                pl.BlockSpec((2, D, COLS), lambda i, place: (0, 0, 0)),
                own((1, SMALL)),
            ],
            scratch_shapes=[
                kept((2, t, D), F32),
                kept((2, t, 1), F32),
                kept((2, t, D), BF),
                kept((2, 2, t, QKV), BF),
                kept((2, 6, t, t), F32),
                kept((2, 2, t, EH), BF),
                kept((2, t, D), F32),
                kept((2, t, D), F32),
                kept((2, t, 1), F32),
                kept((2, t, D), BF),
                kept((2, 2, t, FH), F32),
                kept((2, 2, t, FH), BF),
                kept((2, t, D), F32),
                kept((2, 8, 6 * D), F32),
                kept((2, t, FH), BF),
                kept((2, t, QKV), BF),
                kept((t, D), F32),
                kept((2, D, COLS) if latents > 1 else (8, 128), F32),
            ],
        ),
        out_shape=(
            jax.ShapeDtypeStruct((latents, t, D), BF),
            jax.ShapeDtypeStruct((latents, t, D), F32),
            jax.ShapeDtypeStruct((2, D, COLS), BF),
            jax.ShapeDtypeStruct((latents, 1, SMALL), F32),
        ),
        compiler_params=pltpu.CompilerParams(vmem_limit_bytes=58 * 1024 * 1024),
        cost_estimate=pl.CostEstimate(
            flops=12_000_000_000, bytes_accessed=16_000_000, transcendentals=2_000_000
        ),
    )(place, x, cond, g, w, bm, bqkv, bo, bu, bd)


def swapped(value, axis):
    return lax.ppermute(value, axis, [(0, 1), (1, 0)])


def both_halves(mine, other, half):
    first = jnp.where(half == 0, mine, other)
    second = jnp.where(half == 0, other, mine)
    return jnp.concatenate([first, second], axis=0)


def per_device(
    inputs,
    conditioning,
    out_grad,
    weight_mod,
    bias_mod,
    weight_qkv,
    bias_qv,
    weight_out,
    bias_out,
    first_feed_weight,
    first_feed_bias,
    second_feed_weight,
    second_feed_bias,
):
    section = lax.axis_index("pipe")
    half = lax.axis_index("heads")
    shard = lax.axis_index("shard")
    shards = lax.axis_size("shard")
    rows = weight_qkv.shape[1]
    latents = inputs.shape[0] // 2

    own_mod = lax.dynamic_slice_in_dim(weight_mod[0].reshape(rows, 2 * MODH), half * MODH, MODH, 1)
    own_bias = jnp.concatenate(
        [
            bias_mod.reshape(-1),
            bias_qv.reshape(-1),
            bias_out.reshape(-1),
            first_feed_bias.reshape(-1),
            second_feed_bias.reshape(-1),
        ]
    ).reshape(rows, BIAS_COLS)
    packed = jnp.concatenate(
        [
            weight_qkv.reshape(rows, QKV),
            weight_out[0].T,
            first_feed_weight[0],
            second_feed_weight[0].T,
            own_mod,
            own_bias,
            jnp.zeros((rows, PAD - BIAS_COLS), BF),
        ],
        axis=1,
    )
    gathered = gather_weights(packed)
    w = gathered.reshape(2, 2, shards * rows, WIDE)
    bias = (
        w[:, :, :, COLS + MODH : COLS + MODH + BIAS_COLS]
        .astype(F32)
        .reshape(2, 2, shards, rows * BIAS_COLS)
    )
    own_qv, own_up = EH // shards, FH // shards
    cut = [6 * rows, 2 * own_qv, rows, own_up, rows]
    ends = [sum(cut[: i + 1]) for i in range(5)]
    bm, bqv, bo, bu, bd = jnp.split(bias, ends[:-1], axis=-1)
    bm = bm[:, 0].reshape(2, shards, 6, rows).swapaxes(1, 2).reshape(2, 1, 6 * D)
    bqv = bqv.reshape(2, 2, shards, 2, own_qv).swapaxes(2, 3).reshape(2, 2, 2, EH)
    bqkv = jnp.concatenate([bqv[:, :, :1], jnp.zeros_like(bqv[:, :, :1]), bqv[:, :, 1:]], axis=2)
    bqkv = bqkv.reshape(2, 2, 1, QKV)
    bo = bo[:, 0].reshape(2, 1, D)
    bu = bu.reshape(2, 2, 1, FH)
    bd = bd[:, 0].reshape(2, 1, D)

    place = jnp.stack([section, half]).astype(jnp.int32)
    act, grad, dw, small = run_blocks(
        place,
        inputs,
        conditioning.astype(F32)[:, None, :],
        out_grad,
        w,
        bm,
        bqkv,
        bo,
        bu,
        bd,
        latents,
    )
    padded = -(-SMALL // 1024) * 1024
    small = jnp.pad(small.reshape(latents, SMALL), ((0, 0), (0, padded - SMALL)))
    total, small, sibling, act_other, grad_other = exchange(
        dw.reshape(2, shards, rows, COLS),
        small.reshape(latents, padded // 128, 128),
        act,
        grad.astype(BF),
    )
    activations = both_halves(act, act_other, half)[None]
    input_grads = both_halves(grad, grad_other.astype(F32), half)[None]

    small = small.reshape(2, shards, latents, padded)
    sibling = sibling.reshape(2, latents, padded)
    cond_at = SMALL - 2 * D
    cond_grad = lax.dynamic_index_in_dim(small, shard, 1, keepdims=False) + sibling
    cond_grad = cond_grad[..., cond_at : cond_at + D].reshape(2 * latents, D)
    mine = small.reshape(-1, padded)
    mod_grad = mine[:, : 6 * D].astype(BF)
    cond_act = lax.dynamic_slice_in_dim(mine[:, SMALL - D : SMALL], shard * rows, rows, 1).astype(BF)
    grad_mod = dot_tn(cond_act, mod_grad).reshape(1, rows, 6, D)
    sums = mine[:, : cond_at].sum(axis=0)
    grad_bias_mod = lax.dynamic_slice_in_dim(sums[: 6 * D].reshape(6, D), shard * rows, rows, 1)
    at = 6 * D
    proj = sums[at : at + 2 * QKV].reshape(2, 3, EH)
    proj = lax.dynamic_index_in_dim(proj, half, 0, keepdims=False)
    proj = lax.dynamic_slice_in_dim(proj, shard * own_qv, own_qv, 1)
    grad_bias_qv = jnp.stack([proj[0], proj[2]])
    at += 2 * QKV
    grad_bias_out = lax.dynamic_slice_in_dim(sums, at + shard * rows, rows)
    at += D
    grad_bias_up = lax.dynamic_slice_in_dim(sums, at + half * FH + shard * own_up, own_up)
    at += 2 * FH
    grad_bias_down = lax.dynamic_slice_in_dim(sums, at + shard * rows, rows)

    at = QKV + EH
    return (
        activations,
        input_grads,
        cond_grad,
        grad_mod,
        grad_bias_mod[None],
        total[:, :QKV].reshape(1, rows, 3, EH),
        grad_bias_qv[None],
        total[:, QKV:at].T[None],
        grad_bias_out[None],
        total[:, at : at + FH][None],
        grad_bias_up[None],
        total[:, at + FH :].T[None],
        grad_bias_down[None],
    )


def ring_place():
    shards = lax.axis_size("shard")
    shard = lax.axis_index("shard")
    return jnp.where(shard % 2 == 0, shard // 2, shards - 1 - shard // 2)


def ring_shard(position):
    shards = lax.axis_size("shard")
    position = lax.rem(position + 2 * shards, shards)
    return jnp.where(position < shards // 2, 2 * position, 2 * (shards - 1 - position) + 1)


def greet(devices):
    barrier = pltpu.get_barrier_semaphore()
    for device in devices:
        pl.semaphore_signal(
            barrier, inc=1, device_id=device, device_id_type=pl.DeviceIdType.MESH
        )
    pl.semaphore_wait(barrier, len(devices))


def neighbours():
    r = ring_place()
    return (
        {"shard": ring_shard(r + 1)},
        {"shard": ring_shard(r - 1)},
        {"heads": 1 - lax.axis_index("heads")},
        {"pipe": 1 - lax.axis_index("pipe")},
    )


def remote(src, dst, send, recv, device):
    copy = pltpu.make_async_remote_copy(
        src_ref=src,
        dst_ref=dst,
        send_sem=send,
        recv_sem=recv,
        device_id=device,
        device_id_type=pl.DeviceIdType.MESH,
    )
    return copy


def gather_kernel(shards, split, packed, out, own_sem, send, recv):
    p, h = lax.axis_index("pipe"), lax.axis_index("heads")
    r = ring_place()
    after, before, across, core = neighbours()
    forward_hops, back_hops = shards // 2, shards // 2 - 1
    greet([after, before, across, core])

    def chunk(half, away):
        return out.at[p, half, ring_shard(r - away)]

    def part(half, away, a, b):
        return out.at[p, half, ring_shard(r - away), :, a:b]

    started = []

    def go(ref, kind, sem_at, device):
        copy = remote(ref, ref, send.at[kind, sem_at], recv.at[kind, sem_at], device)
        copy.start()
        started.append(copy)

    def wait_for(ref, kind, sem_at):
        remote(ref, ref, send.at[kind, sem_at], recv.at[kind, sem_at], core).wait_recv()

    def along(half, away, a, b, kind):
        if 0 <= away < forward_hops:
            go(part(half, away, a, b), kind, (away + 1) % shards, after)
        if -back_hops < away <= 0:
            go(part(half, away, a, b), kind, (away - 1) % shards, before)

    own = pltpu.make_async_copy(packed, chunk(h, 0), own_sem)
    own.start()
    own.wait()
    order = [0]
    for k in range(1, forward_hops + 1):
        order += [k] + ([-k] if k <= back_hops else [])
    for away in order:
        if away != 0:
            wait_for(chunk(h, away), 0, away % shards)
        if away == 0:
            go(part(h, 0, split, WIDE), 3, 0, across)
        along(h, away, 0, WIDE, 0)
        go(part(h, away, 0, split), 2, away % shards, across)
        go(chunk(h, away), 4, away % shards, core)
        if away == 0:
            wait_for(part(1 - h, 0, split, WIDE), 3, 0)
        else:
            wait_for(part(1 - h, away, split, WIDE), 1, away % shards)
        along(1 - h, away, split, WIDE, 1)
    for away in order:
        wait_for(part(1 - h, away, 0, split), 2, away % shards)
        go(chunk(1 - h, away), 5, away % shards, core)
    for away in order:
        for kind, half in ((4, h), (5, 1 - h)):
            ref = out.at[1 - p, half, ring_shard(r - away)]
            wait_for(ref, kind, away % shards)
    for copy in started:
        copy.wait_send()


def gather_weights(packed):
    shards = lax.axis_size("shard")

    def kernel(*refs):
        gather_kernel(shards, 16 * 128, *refs)

    return pl.pallas_call(
        kernel,
        in_specs=[pl.BlockSpec(memory_space=pl.ANY)],
        out_specs=pl.BlockSpec(memory_space=pl.ANY),
        out_shape=jax.ShapeDtypeStruct((2, 2, shards) + packed.shape, BF),
        scratch_shapes=[
            pltpu.SemaphoreType.DMA,
            pltpu.SemaphoreType.DMA((6, shards)),
            pltpu.SemaphoreType.DMA((6, shards)),
        ],
        compiler_params=pltpu.CompilerParams(collective_id=1, has_side_effects=True),
    )(packed)


def exchange_kernel(
    shards, dw, small, act, grad, total, smalls, siblings, act_other, grad_other,
    slots, moving, crossing, crossed, send, recv,
):
    h = lax.axis_index("heads")
    r = ring_place()
    after, before, across, core = neighbours()
    forward_hops, back_hops = shards // 2, shards // 2 - 1
    greet([after, before, across, core])
    started = []

    def go(src, dst, kind, at, device):
        copy = remote(src, dst, send.at[kind, at], recv.at[kind, at], device)
        copy.start()
        started.append(copy)

    def wait_for(ref, kind, at):
        remote(ref, ref, send.at[kind, at], recv.at[kind, at], core).wait_recv()

    def own_part(half, away):
        return dw.at[half, ring_shard(r + away)]

    ways = [(after, forward_hops, 1, 0), (before, back_hops, -1, forward_hops)]
    for half in range(2):
        for device, hops, sign, first in ways:
            go(own_part(half, sign * hops), slots.at[first, half], half, first, device)
    go(small, smalls.at[h, ring_shard(r)], 2, 1, after)
    go(small, smalls.at[h, ring_shard(r)], 2, shards - 1, before)
    go(small, smalls.at[h, ring_shard(r)], 3, 0, across)
    go(act, act_other, 4, 0, across)
    go(grad, grad_other, 4, 1, across)
    smalls[h, ring_shard(r)] = small[...]
    for hop in range(forward_hops):
        for half in range(2):
            for device, hops, sign, first in ways:
                if hop < hops - 1:
                    at = first + hop
                    wait_for(slots.at[at, half], half, at)
                    moving[at, half] = (
                        slots[at, half].astype(F32)
                        + own_part(half, sign * (hops - 1 - hop))[...].astype(F32)
                    ).astype(BF)
                    go(moving.at[at, half], slots.at[at + 1, half], half, at + 1, device)
        for away, device in ((hop + 1, after), (-hop - 1, before)):
            hops = forward_hops if away > 0 else back_hops
            if abs(away) <= hops:
                row = smalls.at[h, ring_shard(r - away)]
                wait_for(row, 2, away % shards)
                if abs(away) < hops:
                    go(row, row, 2, (away + (1 if away > 0 else -1)) % shards, device)
                go(row, row, 3, away % shards, across)
    ends = [forward_hops - 1, shards - 2]
    for half in range(2):
        for at in ends:
            wait_for(slots.at[at, half], half, at)

    def summed(half):
        value = dw[half, ring_shard(r)].astype(F32)
        for at in ends:
            value = value + slots[at, half].astype(F32)
        return value

    crossing[...] = summed(1 - h).astype(BF)
    go(crossing, crossed, 4, 2, across)
    for away in range(shards):
        wait_for(smalls.at[1 - h, ring_shard(r - away)], 3, away)
    for half in range(2):
        go(smalls.at[half, ring_shard(r)], siblings.at[half], 5, half, core)
    total[...] = summed(h)
    wait_for(crossed, 4, 2)
    total[...] += crossed[...].astype(F32)
    wait_for(act_other, 4, 0)
    wait_for(grad_other, 4, 1)
    for half in range(2):
        wait_for(siblings.at[half], 5, half)
    for copy in started:
        copy.wait_send()


def exchange(dw, small, act, grad):
    shards = dw.shape[1]
    part = dw.shape[2:]

    def kernel(*refs):
        exchange_kernel(shards, *refs)

    vmem = pl.BlockSpec(memory_space=pltpu.VMEM)
    return pl.pallas_call(
        kernel,
        in_specs=[vmem] * 4,
        out_specs=[vmem] * 5,
        out_shape=(
            jax.ShapeDtypeStruct(part, F32),
            jax.ShapeDtypeStruct((2, shards) + small.shape, F32),
            jax.ShapeDtypeStruct((2,) + small.shape, F32),
            jax.ShapeDtypeStruct(act.shape, BF),
            jax.ShapeDtypeStruct(grad.shape, BF),
        ),
        scratch_shapes=[
            pltpu.VMEM((shards - 1, 2) + part, BF),
            pltpu.VMEM((shards - 1, 2) + part, BF),
            pltpu.VMEM(part, BF),
            pltpu.VMEM(part, BF),
            pltpu.SemaphoreType.DMA((6, shards)),
            pltpu.SemaphoreType.DMA((6, shards)),
        ],
        compiler_params=pltpu.CompilerParams(
            collective_id=2, has_side_effects=True, vmem_limit_bytes=50 * 1024 * 1024
        ),
    )(dw, small, act, grad)


def solution(mesh):
    return jax.shard_map(
        per_device,
        mesh=mesh,
        in_specs=(
            P("shard", None, None),
            P("shard", None),
            P("shard", None, None),
            P("pipe", "shard", None, None),
            P("pipe", None, "shard"),
            P("pipe", "shard", None, "heads"),
            P("pipe", None, ("heads", "shard")),
            P("pipe", "heads", "shard"),
            P("pipe", "shard"),
            P("pipe", "shard", "heads"),
            P("pipe", ("heads", "shard")),
            P("pipe", "heads", "shard"),
            P("pipe", "shard"),
        ),
        out_specs=(
            P("pipe", "shard", None, None),
            P("pipe", "shard", None, None),
            P("shard", None),
            P("pipe", "shard", None, None),
            P("pipe", None, "shard"),
            P("pipe", "shard", None, "heads"),
            P("pipe", None, ("heads", "shard")),
            P("pipe", "heads", "shard"),
            P("pipe", "shard"),
            P("pipe", "shard", "heads"),
            P("pipe", ("heads", "shard")),
            P("pipe", "heads", "shard"),
            P("pipe", "shard"),
        ),
        check_vma=False,
    )
```

```python
import math

import jax
import jax.numpy as jnp
from jax import lax
from jax.experimental import pallas as pl
from jax.experimental.pallas import tpu as pltpu
from jax.sharding import PartitionSpec as P

HD = 64
D = 384
EH = 192
FH = 768
QKV = 3 * EH
COLS = QKV + EH + 2 * FH
MODH = 3 * D
PAD = 128
WIDE = COLS + MODH + PAD
BIAS_COLS = 11
SCALING = HD**-0.5
SMALL = 6 * D + 2 * QKV + D + 2 * FH + D + D + D
BF = jnp.bfloat16
F32 = jnp.float32


def dot_nn(a, b):
    return lax.dot_general(a, b, (((1,), (0,)), ((), ())), preferred_element_type=F32)


def dot_nt(a, b):
    return lax.dot_general(a, b, (((1,), (1,)), ((), ())), preferred_element_type=F32)


def dot_tn(a, b):
    return lax.dot_general(a, b, (((0,), (0,)), ((), ())), preferred_element_type=F32)


def rows_mean(v):
    return jnp.mean(v, axis=-1, keepdims=True)


def norm_rows(v):
    centered = v - rows_mean(v)
    inverse = lax.rsqrt(rows_mean(centered * centered) + 1e-06)
    return centered * inverse, inverse


def norm_back(e, normed, inverse):
    return inverse * (e - rows_mean(e) - normed * rows_mean(e * normed))


def token_sum(v):
    return jnp.sum(v, axis=0, keepdims=True)


def block_kernel(
    latents,
    place,
    x_ref,
    cond_ref,
    g_ref,
    w_ref,
    bm_ref,
    bqkv_ref,
    bo_ref,
    bu_ref,
    bd_ref,
    act_out,
    grad_out,
    dw_out,
    small_out,
    n1_s,
    inv1_s,
    normed_s,
    qkv_s,
    probs_s,
    mixed_s,
    attended_s,
    n2_s,
    inv2_s,
    normed_two_s,
    slope_s,
    activated_s,
    down_s,
    mod_s,
    upg_s,
    pjg_s,
    back_s,
    dw_s,
):
    section = place[0]
    cond = cond_ref[0]
    sig = jax.nn.sigmoid(cond)
    cond_act = (cond * sig).astype(BF)
    cond_rows = jnp.broadcast_to(cond_act, (16, D))

    def weight(s, h, a, b):
        return w_ref[s, h, :, a:b]

    def forward(s, x):
        for h in range(2):
            rows = dot_nn(cond_rows, weight(s, h, COLS, COLS + MODH))[0:1]
            mod_s[s, 0:1, h * MODH : (h + 1) * MODH] = rows + bm_ref[s, :, h * MODH : (h + 1) * MODH]
        shift1, scale1, gate1, shift2, scale2, gate2 = (
            mod_s[s, 0:1, i * D : (i + 1) * D] for i in range(6)
        )
        n1, inv1 = norm_rows(x)
        n1_s[s] = n1
        inv1_s[s] = inv1
        normed = (n1 * (1.0 + scale1) + shift1).astype(BF)
        normed_s[s] = normed
        attended = jnp.broadcast_to(bo_ref[s], x.shape)
        for h in range(2):
            qkv = (dot_nn(normed, weight(s, h, 0, QKV)) + bqkv_ref[s, h]).astype(BF)
            qkv_s[s, h] = qkv
            mixed = []
            for i in range(3):
                q, k, v = (qkv[:, j * EH + i * HD : j * EH + (i + 1) * HD] for j in range(3))
                scores = dot_nt(q, k) * SCALING
                expo = jnp.exp(scores - jnp.max(scores, axis=-1, keepdims=True))
                probs = expo / jnp.sum(expo, axis=-1, keepdims=True)
                probs_s[s, 3 * h + i] = probs
                mixed.append(dot_nn(probs.astype(BF), v))
            mixed = jnp.concatenate(mixed, axis=1).astype(BF)
            mixed_s[s, h] = mixed
            attended = attended + dot_nt(mixed, weight(s, h, QKV, QKV + EH))
        attended_s[s] = attended
        hidden = x + gate1 * attended
        n2, inv2 = norm_rows(hidden)
        n2_s[s] = n2
        inv2_s[s] = inv2
        normed_two = (n2 * (1.0 + scale2) + shift2).astype(BF)
        normed_two_s[s] = normed_two
        down = jnp.broadcast_to(bd_ref[s], x.shape)
        at = QKV + EH
        for h in range(2):
            up = dot_nn(normed_two, weight(s, h, at, at + FH)) + bu_ref[s, h]
            c = math.sqrt(2.0 / math.pi)
            square = up * up
            tanh = jnp.tanh(c * (up + 0.044715 * (square * up)))
            half = 0.5 * (1.0 + tanh)
            activated = (up * half).astype(BF)
            activated_s[s, h] = activated
            slope_s[s, h] = half + (0.5 * c) * up * (1.0 - tanh * tanh) * (
                1.0 + (3 * 0.044715) * square
            )
            down = down + dot_nt(activated, weight(s, h, at + FH, at + 2 * FH))
        down_s[s] = down
        return hidden + gate2 * down

    def add_weight(h, a, b, value):
        if latents == 1:
            dw_out[h, :, a:b] = value.astype(BF)
        else:
            dw_s[h, :, a:b] += value

    def backward(s, g):
        shift1, scale1, gate1, shift2, scale2, gate2 = (
            mod_s[s, 0:1, i * D : (i + 1) * D] for i in range(6)
        )
        at = QKV + EH
        down_grad = (gate2 * g).astype(BF)
        n2_grad = None
        for h in range(2):
            active_grad = dot_nn(down_grad, weight(s, h, at + FH, at + 2 * FH))
            up_grad = (active_grad * slope_s[s, h]).astype(BF)
            upg_s[h] = up_grad
            part = dot_nt(up_grad, weight(s, h, at, at + FH))
            n2_grad = part if n2_grad is None else n2_grad + part
        n2 = n2_s[s]
        hidden_grad = g + norm_back(n2_grad * (1.0 + scale2), n2, inv2_s[s])
        attend_grad = (gate1 * hidden_grad).astype(BF)
        n1_grad = None
        for h in range(2):
            mixed_grad = dot_nn(attend_grad, weight(s, h, QKV, QKV + EH)).astype(BF)
            qkv = qkv_s[s, h]
            parts = [[], [], []]
            for i in range(3):
                q, k, v = (qkv[:, j * EH + i * HD : j * EH + (i + 1) * HD] for j in range(3))
                mg = mixed_grad[:, i * HD : (i + 1) * HD]
                probs = probs_s[s, 3 * h + i]
                parts[2].append(dot_tn(probs.astype(BF), mg))
                weighted = probs * dot_nt(mg, v)
                score_grad = (
                    weighted - probs * jnp.sum(weighted, axis=-1, keepdims=True)
                ).astype(BF)
                parts[0].append(dot_nn(score_grad, k) * SCALING)
                parts[1].append(dot_tn(score_grad, q) * SCALING)
            proj_grad = jnp.concatenate(parts[0] + parts[1] + parts[2], axis=1).astype(BF)
            pjg_s[h] = proj_grad
            part = dot_nt(proj_grad, weight(s, h, 0, QKV))
            n1_grad = part if n1_grad is None else n1_grad + part
        n1 = n1_s[s]
        input_grad = hidden_grad + norm_back(n1_grad * (1.0 + scale1), n1, inv1_s[s])
        back_s[...] = input_grad

        @pl.when(section == s)
        def _():
            grad_out[0] = input_grad
            mod_grad = jnp.concatenate(
                [
                    token_sum(n1_grad),
                    token_sum(n1_grad * n1),
                    token_sum(hidden_grad * attended_s[s]),
                    token_sum(n2_grad),
                    token_sum(n2_grad * n2),
                    token_sum(g * down_s[s]),
                ],
                axis=1,
            ).astype(BF)
            mod_rows = jnp.broadcast_to(mod_grad, (16, 6 * D))
            silu_grad = sum(
                dot_nt(
                    mod_rows[:, h * MODH : (h + 1) * MODH], weight(s, h, COLS, COLS + MODH)
                )[0:1]
                for h in range(2)
            )
            cond_grad = silu_grad * (sig * (1.0 + cond * (1.0 - sig)))
            pieces = [mod_grad.astype(F32)]
            pieces += [token_sum(pjg_s[h].astype(F32)) for h in range(2)]
            pieces += [token_sum(attend_grad.astype(F32))]
            pieces += [token_sum(upg_s[h].astype(F32)) for h in range(2)]
            pieces += [token_sum(down_grad.astype(F32)), cond_grad, cond_act.astype(F32)]
            small_out[0] = jnp.concatenate(pieces, axis=1)
            for h in range(2):
                add_weight(h, 0, QKV, dot_tn(normed_s[s], pjg_s[h]))
                add_weight(h, QKV, at, dot_tn(attend_grad, mixed_s[s, h]))
                add_weight(h, at, at + FH, dot_tn(normed_two_s[s], upg_s[h]))
                add_weight(h, at + FH, at + 2 * FH, dot_tn(down_grad, activated_s[s, h]))

    if latents > 1:

        @pl.when(pl.program_id(0) == 0)
        def _():
            dw_s[...] = jnp.zeros_like(dw_s)

    y0 = forward(0, x_ref[0].astype(F32)).astype(BF)

    @pl.when(section == 0)
    def _():
        act_out[0] = y0

    y1 = forward(1, y0.astype(F32))

    @pl.when(section == 1)
    def _():
        act_out[0] = y1.astype(BF)

    backward(1, g_ref[0])

    @pl.when(section == 0)
    def _():
        backward(0, back_s[...].astype(BF).astype(F32))

    if latents > 1:

        @pl.when(pl.program_id(0) == latents - 1)
        def _():
            dw_out[...] = dw_s[...].astype(BF)


def run_blocks(place, x, cond, g, w, bm, bqkv, bo, bu, bd, latents):
    length = x.shape[1]

    def picked(shape):
        return pl.BlockSpec(
            (1,) + shape, lambda i, place: (place[1] * latents + i,) + (0,) * len(shape)
        )

    def own(shape):
        return pl.BlockSpec((1,) + shape, lambda i, place: (i,) + (0,) * len(shape))

    def whole(a):
        return pl.BlockSpec(
            a.shape, lambda i, place: (0,) * a.ndim, pipeline_mode=pl.Buffered(1)
        )

    def kept(shape, dtype):
        return pltpu.VMEM(shape, dtype)

    def kernel(*refs):
        block_kernel(latents, *refs)

    t = length
    return pl.pallas_call(
        kernel,
        grid_spec=pltpu.PrefetchScalarGridSpec(
            num_scalar_prefetch=1,
            grid=(latents,),
            in_specs=[picked((t, D)), picked((1, D)), picked((t, D))]
            + [whole(a) for a in (w, bm, bqkv, bo, bu, bd)],
            out_specs=[
                own((t, D)),
                own((t, D)),
                pl.BlockSpec((2, D, COLS), lambda i, place: (0, 0, 0)),
                own((1, SMALL)),
            ],
            scratch_shapes=[
                kept((2, t, D), F32),
                kept((2, t, 1), F32),
                kept((2, t, D), BF),
                kept((2, 2, t, QKV), BF),
                kept((2, 6, t, t), F32),
                kept((2, 2, t, EH), BF),
                kept((2, t, D), F32),
                kept((2, t, D), F32),
                kept((2, t, 1), F32),
                kept((2, t, D), BF),
                kept((2, 2, t, FH), F32),
                kept((2, 2, t, FH), BF),
                kept((2, t, D), F32),
                kept((2, 8, 6 * D), F32),
                kept((2, t, FH), BF),
                kept((2, t, QKV), BF),
                kept((t, D), F32),
                kept((2, D, COLS) if latents > 1 else (8, 128), F32),
            ],
        ),
        out_shape=(
            jax.ShapeDtypeStruct((latents, t, D), BF),
            jax.ShapeDtypeStruct((latents, t, D), F32),
            jax.ShapeDtypeStruct((2, D, COLS), BF),
            jax.ShapeDtypeStruct((latents, 1, SMALL), F32),
        ),
        compiler_params=pltpu.CompilerParams(vmem_limit_bytes=58 * 1024 * 1024),
        cost_estimate=pl.CostEstimate(
            flops=12_000_000_000, bytes_accessed=16_000_000, transcendentals=2_000_000
        ),
    )(place, x, cond, g, w, bm, bqkv, bo, bu, bd)


def swapped(value, axis):
    return lax.ppermute(value, axis, [(0, 1), (1, 0)])


def both_halves(mine, other, half):
    first = jnp.where(half == 0, mine, other)
    second = jnp.where(half == 0, other, mine)
    return jnp.concatenate([first, second], axis=0)


def per_device(
    inputs,
    conditioning,
    out_grad,
    weight_mod,
    bias_mod,
    weight_qkv,
    bias_qv,
    weight_out,
    bias_out,
    first_feed_weight,
    first_feed_bias,
    second_feed_weight,
    second_feed_bias,
):
    section = lax.axis_index("pipe")
    half = lax.axis_index("heads")
    shard = lax.axis_index("shard")
    shards = lax.axis_size("shard")
    rows = weight_qkv.shape[1]
    latents = inputs.shape[0] // 2

    own_mod = lax.dynamic_slice_in_dim(weight_mod[0].reshape(rows, 2 * MODH), half * MODH, MODH, 1)
    own_bias = jnp.concatenate(
        [
            bias_mod.reshape(-1),
            bias_qv.reshape(-1),
            bias_out.reshape(-1),
            first_feed_bias.reshape(-1),
            second_feed_bias.reshape(-1),
        ]
    ).reshape(rows, BIAS_COLS)
    packed = jnp.concatenate(
        [
            weight_qkv.reshape(rows, QKV),
            weight_out[0].T,
            first_feed_weight[0],
            second_feed_weight[0].T,
            own_mod,
            own_bias,
            jnp.zeros((rows, PAD - BIAS_COLS), BF),
        ],
        axis=1,
    )
    gathered = gather_weights(packed)
    w = gathered.reshape(2, 2, shards * rows, WIDE)
    bias = (
        w[:, :, :, COLS + MODH : COLS + MODH + BIAS_COLS]
        .astype(F32)
        .reshape(2, 2, shards, rows * BIAS_COLS)
    )
    own_qv, own_up = EH // shards, FH // shards
    cut = [6 * rows, 2 * own_qv, rows, own_up, rows]
    ends = [sum(cut[: i + 1]) for i in range(5)]
    bm, bqv, bo, bu, bd = jnp.split(bias, ends[:-1], axis=-1)
    bm = bm[:, 0].reshape(2, shards, 6, rows).swapaxes(1, 2).reshape(2, 1, 6 * D)
    bqv = bqv.reshape(2, 2, shards, 2, own_qv).swapaxes(2, 3).reshape(2, 2, 2, EH)
    bqkv = jnp.concatenate([bqv[:, :, :1], jnp.zeros_like(bqv[:, :, :1]), bqv[:, :, 1:]], axis=2)
    bqkv = bqkv.reshape(2, 2, 1, QKV)
    bo = bo[:, 0].reshape(2, 1, D)
    bu = bu.reshape(2, 2, 1, FH)
    bd = bd[:, 0].reshape(2, 1, D)

    place = jnp.stack([section, half]).astype(jnp.int32)
    act, grad, dw, small = run_blocks(
        place,
        inputs,
        conditioning.astype(F32)[:, None, :],
        out_grad,
        w,
        bm,
        bqkv,
        bo,
        bu,
        bd,
        latents,
    )
    padded = -(-SMALL // 1024) * 1024
    small = jnp.pad(small.reshape(latents, SMALL), ((0, 0), (0, padded - SMALL)))
    total, small, sibling, act_other, grad_other = exchange(
        dw.reshape(2, shards, rows, COLS),
        small.reshape(latents, padded // 128, 128),
        act,
        grad.astype(BF),
    )
    activations = both_halves(act, act_other, half)[None]
    input_grads = both_halves(grad, grad_other.astype(F32), half)[None]

    small = small.reshape(2, shards, latents, padded)
    sibling = sibling.reshape(2, latents, padded)
    cond_at = SMALL - 2 * D
    cond_grad = lax.dynamic_index_in_dim(small, shard, 1, keepdims=False) + sibling
    cond_grad = cond_grad[..., cond_at : cond_at + D].reshape(2 * latents, D)
    mine = small.reshape(-1, padded)
    mod_grad = mine[:, : 6 * D].astype(BF)
    cond_act = lax.dynamic_slice_in_dim(mine[:, SMALL - D : SMALL], shard * rows, rows, 1).astype(BF)
    grad_mod = dot_tn(cond_act, mod_grad).reshape(1, rows, 6, D)
    sums = mine[:, : cond_at].sum(axis=0)
    grad_bias_mod = lax.dynamic_slice_in_dim(sums[: 6 * D].reshape(6, D), shard * rows, rows, 1)
    at = 6 * D
    proj = sums[at : at + 2 * QKV].reshape(2, 3, EH)
    proj = lax.dynamic_index_in_dim(proj, half, 0, keepdims=False)
    proj = lax.dynamic_slice_in_dim(proj, shard * own_qv, own_qv, 1)
    grad_bias_qv = jnp.stack([proj[0], proj[2]])
    at += 2 * QKV
    grad_bias_out = lax.dynamic_slice_in_dim(sums, at + shard * rows, rows)
    at += D
    grad_bias_up = lax.dynamic_slice_in_dim(sums, at + half * FH + shard * own_up, own_up)
    at += 2 * FH
    grad_bias_down = lax.dynamic_slice_in_dim(sums, at + shard * rows, rows)

    at = QKV + EH
    return (
        activations,
        input_grads,
        cond_grad,
        grad_mod,
        grad_bias_mod[None],
        total[:, :QKV].reshape(1, rows, 3, EH),
        grad_bias_qv[None],
        total[:, QKV:at].T[None],
        grad_bias_out[None],
        total[:, at : at + FH][None],
        grad_bias_up[None],
        total[:, at + FH :].T[None],
        grad_bias_down[None],
    )


def ring_place():
    shards = lax.axis_size("shard")
    shard = lax.axis_index("shard")
    return jnp.where(shard % 2 == 0, shard // 2, shards - 1 - shard // 2)


def ring_shard(position):
    shards = lax.axis_size("shard")
    position = lax.rem(position + 2 * shards, shards)
    return jnp.where(position < shards // 2, 2 * position, 2 * (shards - 1 - position) + 1)


def greet(devices):
    barrier = pltpu.get_barrier_semaphore()
    for device in devices:
        pl.semaphore_signal(
            barrier, inc=1, device_id=device, device_id_type=pl.DeviceIdType.MESH
        )
    pl.semaphore_wait(barrier, len(devices))


def neighbours():
    r = ring_place()
    return (
        {"shard": ring_shard(r + 1)},
        {"shard": ring_shard(r - 1)},
        {"heads": 1 - lax.axis_index("heads")},
        {"pipe": 1 - lax.axis_index("pipe")},
    )


def remote(src, dst, send, recv, device):
    copy = pltpu.make_async_remote_copy(
        src_ref=src,
        dst_ref=dst,
        send_sem=send,
        recv_sem=recv,
        device_id=device,
        device_id_type=pl.DeviceIdType.MESH,
    )
    return copy


def gather_kernel(shards, split, packed, out, own_sem, send, recv):
    p, h = lax.axis_index("pipe"), lax.axis_index("heads")
    r = ring_place()
    after, before, across, core = neighbours()
    forward_hops, back_hops = shards // 2, shards // 2 - 1
    greet([after, before, across, core])

    def chunk(half, away):
        return out.at[p, half, ring_shard(r - away)]

    def part(half, away, a, b):
        return out.at[p, half, ring_shard(r - away), :, a:b]

    started = []

    def go(ref, kind, sem_at, device, src=None):
        src = ref if src is None else src
        copy = remote(src, ref, send.at[kind, sem_at], recv.at[kind, sem_at], device)
        copy.start()
        started.append(copy)

    def wait_for(ref, kind, sem_at):
        remote(ref, ref, send.at[kind, sem_at], recv.at[kind, sem_at], core).wait_recv()

    def along(half, away, a, b, kind, src=None):
        mid = (a + b) // 2
        if 0 <= away < forward_hops - 1:
            go(part(half, away, a, b), kind, away + 1, after, src)
        elif away == forward_hops - 1:
            go(part(half, away, a, mid), kind, forward_hops, after)
        if -back_hops < away <= 0:
            go(part(half, away, a, b), kind, (away - 1) % shards, before, src)
        elif away == -back_hops:
            go(part(half, away, mid, b), kind, 0, before)

    def arrived(half, away, a, b, kind):
        mid = (a + b) // 2
        if away == forward_hops:
            wait_for(part(half, away, a, mid), kind, forward_hops)
            wait_for(part(half, away, mid, b), kind, 0)
        else:
            wait_for(part(half, away, a, b), kind, away % shards)

    order = [0]
    for k in range(1, forward_hops + 1):
        order += [k] + ([-k] if k <= back_hops else [])
    own = pltpu.make_async_copy(packed, chunk(h, 0), own_sem)
    own.start()
    go(part(h, 0, split, WIDE), 3, 0, across, packed.at[:, split:WIDE])
    along(h, 0, 0, WIDE, 0, packed)
    go(part(h, 0, 0, split), 2, 0, across, packed.at[:, 0:split])
    go(chunk(h, 0), 4, 0, core, packed)
    wait_for(part(1 - h, 0, split, WIDE), 3, 0)
    along(1 - h, 0, split, WIDE, 1)
    for away in order[1:]:
        arrived(h, away, 0, WIDE, 0)
        along(h, away, 0, WIDE, 0)
        go(part(h, away, 0, split), 2, away % shards, across)
        go(chunk(h, away), 4, away % shards, core)
        arrived(1 - h, away, split, WIDE, 1)
        along(1 - h, away, split, WIDE, 1)
    for away in order:
        wait_for(part(1 - h, away, 0, split), 2, away % shards)
        go(chunk(1 - h, away), 5, away % shards, core)
    for away in order:
        for kind, half in ((4, h), (5, 1 - h)):
            ref = out.at[1 - p, half, ring_shard(r - away)]
            wait_for(ref, kind, away % shards)
    own.wait()
    for copy in started:
        copy.wait_send()


def gather_weights(packed):
    shards = lax.axis_size("shard")

    def kernel(*refs):
        gather_kernel(shards, 16 * 128, *refs)

    return pl.pallas_call(
        kernel,
        in_specs=[pl.BlockSpec(memory_space=pl.ANY)],
        out_specs=pl.BlockSpec(memory_space=pl.ANY),
        out_shape=jax.ShapeDtypeStruct((2, 2, shards) + packed.shape, BF),
        scratch_shapes=[
            pltpu.SemaphoreType.DMA,
            pltpu.SemaphoreType.DMA((6, shards)),
            pltpu.SemaphoreType.DMA((6, shards)),
        ],
        compiler_params=pltpu.CompilerParams(collective_id=1, has_side_effects=True),
    )(packed)


def exchange_kernel(
    shards, dw, small, act, grad, total, smalls, siblings, act_other, grad_other,
    slots, moving, crossing, crossed, send, recv,
):
    h = lax.axis_index("heads")
    r = ring_place()
    after, before, across, core = neighbours()
    forward_hops, back_hops = shards // 2, shards // 2 - 1
    greet([after, before, across, core])
    started = []

    def go(src, dst, kind, at, device):
        copy = remote(src, dst, send.at[kind, at], recv.at[kind, at], device)
        copy.start()
        started.append(copy)

    def wait_for(ref, kind, at):
        remote(ref, ref, send.at[kind, at], recv.at[kind, at], core).wait_recv()

    def own_part(half, away):
        return dw.at[half, ring_shard(r + away)]

    mid = COLS // 2
    ways = [(after, 1, 0, 0, mid), (before, -1, forward_hops, mid, COLS)]
    for half in range(2):
        for device, sign, first, a, b in ways:
            src = dw.at[half, ring_shard(r + sign * forward_hops), :, a:b]
            go(src, slots.at[first, half, :, a:b], half, first, device)
    go(small, smalls.at[h, ring_shard(r)], 2, 1, after)
    go(small, smalls.at[h, ring_shard(r)], 2, shards - 1, before)
    go(small, smalls.at[h, ring_shard(r)], 3, 0, across)
    go(act, act_other, 4, 0, across)
    go(grad, grad_other, 4, 1, across)
    smalls[h, ring_shard(r)] = small[...]
    for hop in range(forward_hops):
        for half in range(2):
            for device, sign, first, a, b in ways:
                if hop < forward_hops - 1:
                    at = first + hop
                    own = own_part(half, sign * (forward_hops - 1 - hop))
                    if hop == 0:
                        wait_for(slots.at[at, half, :, a:b], half, at)
                        moving[at, half] = own[...]
                    else:
                        a, b = 0, COLS
                        wait_for(slots.at[at, half], half, at)
                    moving[at, half, :, a:b] = (
                        slots[at, half, :, a:b].astype(F32) + own[:, a:b].astype(F32)
                    ).astype(BF)
                    go(moving.at[at, half], slots.at[at + 1, half], half, at + 1, device)
        for away, device in ((hop + 1, after), (-hop - 1, before)):
            hops = forward_hops if away > 0 else back_hops
            if abs(away) <= hops:
                row = smalls.at[h, ring_shard(r - away)]
                wait_for(row, 2, away % shards)
                if abs(away) < hops:
                    go(row, row, 2, (away + (1 if away > 0 else -1)) % shards, device)
                go(row, row, 3, away % shards, across)
    ends = [forward_hops - 1, 2 * forward_hops - 1]
    for half in range(2):
        for at in ends:
            wait_for(slots.at[at, half], half, at)

    def summed(half):
        value = dw[half, ring_shard(r)].astype(F32)
        for at in ends:
            value = value + slots[at, half].astype(F32)
        return value

    crossing[...] = summed(1 - h).astype(BF)
    go(crossing, crossed, 4, 2, across)
    for away in range(shards):
        wait_for(smalls.at[1 - h, ring_shard(r - away)], 3, away)
    for half in range(2):
        go(smalls.at[half, ring_shard(r)], siblings.at[half], 5, half, core)
    total[...] = summed(h)
    wait_for(crossed, 4, 2)
    total[...] += crossed[...].astype(F32)
    wait_for(act_other, 4, 0)
    wait_for(grad_other, 4, 1)
    for half in range(2):
        wait_for(siblings.at[half], 5, half)
    for copy in started:
        copy.wait_send()


def exchange(dw, small, act, grad):
    shards = dw.shape[1]
    part = dw.shape[2:]

    def kernel(*refs):
        exchange_kernel(shards, *refs)

    vmem = pl.BlockSpec(memory_space=pltpu.VMEM)
    return pl.pallas_call(
        kernel,
        in_specs=[vmem] * 4,
        out_specs=[vmem] * 5,
        out_shape=(
            jax.ShapeDtypeStruct(part, F32),
            jax.ShapeDtypeStruct((2, shards) + small.shape, F32),
            jax.ShapeDtypeStruct((2,) + small.shape, F32),
            jax.ShapeDtypeStruct(act.shape, BF),
            jax.ShapeDtypeStruct(grad.shape, BF),
        ),
        scratch_shapes=[
            pltpu.VMEM((shards, 2) + part, BF),
            pltpu.VMEM((shards, 2) + part, BF),
            pltpu.VMEM(part, BF),
            pltpu.VMEM(part, BF),
            pltpu.SemaphoreType.DMA((6, shards)),
            pltpu.SemaphoreType.DMA((6, shards)),
        ],
        compiler_params=pltpu.CompilerParams(
            collective_id=2, has_side_effects=True, vmem_limit_bytes=50 * 1024 * 1024
        ),
    )(dw, small, act, grad)


def solution(mesh):
    return jax.shard_map(
        per_device,
        mesh=mesh,
        in_specs=(
            P("shard", None, None),
            P("shard", None),
            P("shard", None, None),
            P("pipe", "shard", None, None),
            P("pipe", None, "shard"),
            P("pipe", "shard", None, "heads"),
            P("pipe", None, ("heads", "shard")),
            P("pipe", "heads", "shard"),
            P("pipe", "shard"),
            P("pipe", "shard", "heads"),
            P("pipe", ("heads", "shard")),
            P("pipe", "heads", "shard"),
            P("pipe", "shard"),
        ),
        out_specs=(
            P("pipe", "shard", None, None),
            P("pipe", "shard", None, None),
            P("shard", None),
            P("pipe", "shard", None, None),
            P("pipe", None, "shard"),
            P("pipe", "shard", None, "heads"),
            P("pipe", None, ("heads", "shard")),
            P("pipe", "heads", "shard"),
            P("pipe", "shard"),
            P("pipe", "shard", "heads"),
            P("pipe", ("heads", "shard")),
            P("pipe", "heads", "shard"),
            P("pipe", "shard"),
        ),
        check_vma=False,
    )
```
